32 devices in a mesh: row: 8 (over z, x), col: 4 (over y, core).
Axes of the slice: x: 2, y: 2, z: 4, core: 2. Of those that a mesh axis runs over, the one named last changes fastest.
Arguments:
- features: bfloat16 [4096, 256], P(('row', 'col')), may hold values from -6 to 6
- weight: bfloat16 [256, 256], replicated, may hold values from -0.375 to 0.375
- cotangent: bfloat16 [4096, 256], P(('row', 'col')), may hold values from -6 to 6
- adjacency_tiles: bfloat16 [8, 4, 8, 128, 128], P('row', 'col'), as said below
- tile_coords: int32 [8, 4, 8, 2], P('row', 'col'), may hold values from 0 to 7, as said below
- tile_counts: int32 [8, 4], P('row', 'col'), may hold values from 1 to 8, as said below
Outputs:
- activations: bfloat16 [4096, 256], P(('row', 'col'))
- weight_grad: float32 [256, 256], replicated
- input_grad: bfloat16 [4096, 256], P(('row', 'col'))
The draws below stay inside these ranges and needn't reach their ends.
Inputs may be any that keep to these rules, and one draw needn't show every extreme that they name: `adjacency_tiles`: edge weights are nonnegative. `tile_coords`: entry 0 of a slot is a tile row below 4, entry 1 a tile column below 8; the live slots of one block name distinct tiles. `tile_counts`: some block has exactly 8 live slots.
All inputs are finite; a program needn't handle non-finite values.
Results may differ from the reference program's by a relative error of at most 0.03.
Values may be sent and summed in bfloat16 or wider, within the bound.
No kernel may reach another device: no remote copies, remote signals or barrier semaphores. Data moves between devices by JAX's collectives and lax.ppermute only.
A program may use at most 128 MiB of HBM per device.

```python
import math
import jax
import jax.numpy as jnp
from jax import lax

F = 256
TILE = 128
NODE_DEV = 128
NODES = 4096
TILE_ROWS = 4
TILE_COLS = 8
CAPACITY = 8
N_ROW = 8
N_COL = 4


def draw_adjacency_tiles(key, part):
    key = jax.random.fold_in(key, 11)
    mask_key, value_key, density_key = jax.random.split(key, 3)
    shape = (N_ROW, N_COL, CAPACITY, TILE, TILE)
    lowest_density = max(0.004, 4.0 / (TILE * TILE))
    highest_density = max(0.03, 2.0 * lowest_density)
    spread = jax.random.uniform(density_key, (N_ROW, N_COL, CAPACITY, 1, 1), jnp.float32)
    density = jnp.exp(math.log(lowest_density) + spread * (math.log(highest_density) - math.log(lowest_density)))
    edges = jax.random.uniform(mask_key, shape, jnp.float32) < density
    mean_density = (highest_density - lowest_density) / math.log(highest_density / lowest_density)
    lowest = max(1, CAPACITY // 8)
    highest = max(lowest + 1, CAPACITY // 2 + 1)
    mean_count = 0.5 * (lowest + highest - 1)
    degree = mean_density * TILE * mean_count * N_COL / TILE_ROWS
    scale = 1.0 / math.sqrt(max(degree, 1.0))
    values = jax.random.uniform(value_key, shape, jnp.float32, 0.5, 1.5)
    return jnp.where(edges, values * scale, 0.0).astype(jnp.bfloat16)


def draw_tile_coords(key, part):
    key = jax.random.fold_in(key, 12)
    slots = TILE_ROWS * TILE_COLS
    upper = max(2, 2 ** 30 // slots)
    scores = jax.random.randint(key, (N_ROW, N_COL, slots), 0, upper) * slots + jnp.arange(slots, dtype=jnp.int32)
    chosen = jnp.argsort(scores, axis=-1, stable=True)[..., :CAPACITY].astype(jnp.int32)
    return jnp.stack([chosen // TILE_COLS, chosen % TILE_COLS], axis=-1).astype(jnp.int32)


def draw_tile_counts(key, part):
    key = jax.random.fold_in(key, 13)
    base_key, pick_key = jax.random.split(key)
    lowest = max(1, CAPACITY // 8)
    highest = max(lowest + 1, CAPACITY // 2 + 1)
    base = jax.random.randint(base_key, (N_ROW, N_COL), lowest, highest)
    picked = jax.random.randint(pick_key, (), 0, N_ROW * N_COL)
    position = jnp.arange(N_ROW * N_COL, dtype=jnp.int32).reshape(N_ROW, N_COL)
    return jnp.where(position == picked, CAPACITY, base).astype(jnp.int32)


def shard_levels(own_key, extent, cuts, least, high):
    gain, own = 1.0, jax.random.fold_in(own_key, 6)
    for dim, parts in cuts:
        draws = jnp.exp(jax.random.uniform(jax.random.fold_in(own, dim), (parts,), jnp.float32, least / len(cuts), high / len(cuts)))
        gain = gain * jnp.repeat(draws, extent[dim] // parts).reshape([-1 if axis == dim else 1 for axis in range(len(extent))])
    return gain


def bell_draw(stream_key, dims, scale, reach, cuts=(), held_as=jnp.bfloat16):
    values = scale * jax.random.normal(stream_key, dims, jnp.float32)
    if cuts:
        values = values * shard_levels(stream_key, dims, cuts, -0.22, 0.18)
    return jnp.clip(values, -reach, reach).astype(held_as)


def setup_inputs(seed: int = 0) -> dict:
    key_list = jax.random.split(jax.random.key(seed), 7)
    features = bell_draw(key_list[0], (NODES, F), 1.0, 6.0, ((0, 32),))
    weight = bell_draw(key_list[1], (F, F), F ** -0.5, 0.375)
    cotangent = bell_draw(key_list[2], (NODES, F), 1.0, 6.0, ((0, 32),))
    adjacency_tiles = draw_adjacency_tiles(jax.random.fold_in(key_list[6], 71), 0)
    tile_coords = draw_tile_coords(jax.random.fold_in(key_list[6], 71), 0)
    tile_counts = draw_tile_counts(jax.random.fold_in(key_list[6], 71), 0)
    return {"features": features, "weight": weight, "cotangent": cotangent, "adjacency_tiles": adjacency_tiles, "tile_coords": tile_coords, "tile_counts": tile_counts}


def tile_sum(totals, adjacency, coordinates, live_count, source, flipped):
    def advance(index, running):
        block = lax.dynamic_index_in_dim(adjacency, index, 0, keepdims=False)
        tile_row = coordinates[index, 0]
        tile_col = coordinates[index, 1]
        if flipped:
            picked = lax.dynamic_index_in_dim(source, tile_row, 0, keepdims=False)
            term = jnp.dot(block.T, picked, preferred_element_type=jnp.float32)
            return running.at[tile_col].add(term)
        picked = lax.dynamic_index_in_dim(source, tile_col, 0, keepdims=False)
        term = jnp.dot(block, picked, preferred_element_type=jnp.float32)
        return running.at[tile_row].add(term)
    return lax.fori_loop(0, live_count, advance, totals)


def reference(features, weight, cotangent, adjacency_tiles, tile_coords, tile_counts):
    node_blocks = features.reshape(N_ROW, N_COL, NODE_DEV, F)

    def row_block(row_index):
        def over_col(total, col_index):
            source = lax.dynamic_index_in_dim(node_blocks, col_index, 1, keepdims=False)
            source = source.reshape(TILE_COLS, TILE, F)
            part = tile_sum(jnp.zeros((TILE_ROWS, TILE, F), jnp.float32),
                            adjacency_tiles[row_index, col_index], tile_coords[row_index, col_index],
                            tile_counts[row_index, col_index], source, False)
            rounded = lax.optimization_barrier(part.astype(jnp.bfloat16))
            return total + rounded.astype(jnp.float32), None
        total, _ = lax.scan(over_col, jnp.zeros((TILE_ROWS, TILE, F), jnp.float32), jnp.arange(N_COL))
        return total

    aggregated = lax.map(row_block, jnp.arange(N_ROW)).reshape(NODES, F).astype(jnp.bfloat16)
    preact = jnp.dot(aggregated, weight, preferred_element_type=jnp.float32)
    sigmoid_z = jax.nn.sigmoid(preact)
    activations = (preact * sigmoid_z).astype(jnp.bfloat16)
    grad_pre = (cotangent.astype(jnp.float32) * sigmoid_z * (1.0 + preact * (1.0 - sigmoid_z))).astype(jnp.bfloat16)
    weight_grad = lax.dot_general(aggregated, grad_pre, (((0,), (0,)), ((), ())), preferred_element_type=jnp.float32)
    grad_agg = lax.dot_general(grad_pre, weight, (((1,), (1,)), ((), ())), preferred_element_type=jnp.float32).astype(jnp.bfloat16)
    grad_rows = grad_agg.reshape(N_ROW, TILE_ROWS, TILE, F)

    def col_block(col_index):
        def over_row(total, row_index):
            source = lax.dynamic_index_in_dim(grad_rows, row_index, 0, keepdims=False)
            part = tile_sum(jnp.zeros((TILE_COLS, TILE, F), jnp.float32),
                            adjacency_tiles[row_index, col_index], tile_coords[row_index, col_index],
                            tile_counts[row_index, col_index], source, True)
            rounded = lax.optimization_barrier(part.astype(jnp.bfloat16))
            return total + rounded.astype(jnp.float32), None
        total, _ = lax.scan(over_row, jnp.zeros((TILE_COLS, TILE, F), jnp.float32), jnp.arange(N_ROW))
        return total

    columns = lax.map(col_block, jnp.arange(N_COL)).reshape(N_COL, N_ROW, NODE_DEV, F)
    input_grad = jnp.transpose(columns, (1, 0, 2, 3)).reshape(NODES, F).astype(jnp.bfloat16)
    return activations, weight_grad, input_grad
```

```python
import functools

import jax
import jax.numpy as jnp
from jax import lax
from jax.experimental import pallas as pl
from jax.experimental.pallas import tpu as pltpu
from jax.sharding import PartitionSpec as P

F32 = jnp.float32
BF16 = jnp.bfloat16
VMEM = pl.BlockSpec(memory_space=pltpu.VMEM)
SMEM = pl.BlockSpec(memory_space=pltpu.SMEM)
VMEM_LIMIT = 16 * 1024 * 1024


def swap(value, axis, bits):
    size = lax.axis_size(axis)
    return lax.ppermute(value, axis, [(i, i ^ bits) for i in range(size)])


def call(kernel, outs, in_specs, scratch=(), flops=0):
    return pl.pallas_call(
        kernel,
        out_shape=outs,
        in_specs=in_specs,
        out_specs=jax.tree.map(lambda _: VMEM, outs),
        scratch_shapes=list(scratch),
        compiler_params=pltpu.CompilerParams(vmem_limit_bytes=VMEM_LIMIT),
        cost_estimate=pl.CostEstimate(flops=flops, bytes_accessed=0, transcendentals=0),
    )


def shape(rows, width, dtype=BF16):
    return jax.ShapeDtypeStruct((rows, width), dtype)


def block(ref, k, tile):
    return ref[k * tile:(k + 1) * tile, :]


def tile_loop(coords, count, tiles, source, total, flipped):
    row, col = lax.axis_index("row"), lax.axis_index("col")
    total[...] = jnp.zeros_like(total)

    def step(s, carry):
        r = coords[0, 0, s, 0] ^ col
        c = coords[0, 0, s, 1] ^ row
        if flipped:
            total[c] += lax.dot_general(
                tiles[0, 0, s], source[r], (((0,), (0,)), ((), ())), preferred_element_type=F32
            )
        else:
            total[r] += jnp.dot(tiles[0, 0, s], source[c], preferred_element_type=F32)
        return carry

    lax.fori_loop(0, count[0, 0], step, 0)


def forward_kernel(coords, count, tiles, *refs, tile):
    parts, (keep, send, source, total) = refs[:-4], refs[-4:]
    for slot, part in enumerate(parts):
        source[slot] = part[...]
    tile_loop(coords, count, tiles, source, total, False)
    for k in range(total.shape[0] // 2):
        keep[k * tile:(k + 1) * tile, :] = total[2 * k].astype(BF16)
        send[k * tile:(k + 1) * tile, :] = total[2 * k + 1].astype(BF16)


def backward_kernel(coords, count, tiles, mine, other, keep, send, source, total, *, tile):
    for k in range(source.shape[0] // 2):
        source[2 * k] = block(mine, k, tile)
        source[2 * k + 1] = block(other, k, tile)
    tile_loop(coords, count, tiles, source, total, True)
    for k in range(total.shape[0] // 2):
        keep[k * tile:(k + 1) * tile, :] = total[2 * k].astype(BF16)
        send[k * tile:(k + 1) * tile, :] = total[2 * k + 1].astype(BF16)


def add_kernel(a, b, out, *, flip, tile):
    for k in range(out.shape[0] // tile):
        total = block(a, k, tile).astype(F32) + block(b, k ^ flip, tile).astype(F32)
        out[k * tile:(k + 1) * tile, :] = total.astype(BF16)


def split_kernel(a, b, *outs, tile):
    for k, out in enumerate(outs):
        out[...] = (block(a, k, tile).astype(F32) + block(b, k, tile).astype(F32)).astype(BF16)


def sum_kernel(*refs):
    total = refs[0][...].astype(F32)
    for ref in refs[1:-1]:
        total += ref[...].astype(F32)
    refs[-1][...] = total.astype(refs[-1].dtype)


def dense_kernel(half, other, weight, *refs, flip, tile, share):
    cots, (act, out, kept, agg, gpre) = refs[:-5], refs[-5:]
    blocks = len(cots)
    add_kernel(half, other, agg, flip=flip, tile=tile)
    col = lax.axis_index("col")
    for k in range(blocks):
        rows = slice(k * tile, (k + 1) * tile)
        pre = jnp.dot(agg[rows, :], weight[...], preferred_element_type=F32)
        sig = jax.nn.sigmoid(pre)
        if k == 0:
            act[...] = (pre * sig).astype(BF16)
        gpre[rows, :] = (cots[k][...].astype(F32) * sig * (1.0 + pre * (1.0 - sig))).astype(BF16)
    grad = lax.dot_general(
        gpre[...], weight[...], (((1,), (1,)), ((), ())), preferred_element_type=F32
    )
    out[:blocks * tile, :] = grad.astype(BF16)
    full = lax.dot_general(
        agg[...], gpre[...], (((0,), (0,)), ((), ())), preferred_element_type=F32
    ).astype(BF16)
    wide = full.shape[0] // share
    for j in range(wide):
        @pl.when(col == j)
        def _():
            kept[...] = full[j * share:(j + 1) * share, :]
            peer = j ^ 1
            out[blocks * tile:, :] = full[peer * share:(peer + 1) * share, :]


def place_kernel(*refs, share):
    parts, out = refs[:-1], refs[-1]
    col = lax.axis_index("col")
    for slot, part in enumerate(parts):
        start = pl.multiple_of((col ^ slot) * share, share)
        out[pl.ds(start, share), :] = part[...].astype(F32)


def body(features, weight, cotangent, adjacency_tiles, tile_coords, tile_counts):
    tile, width = features.shape
    n_row, n_col = lax.axis_size("row"), lax.axis_size("col")
    half = n_col // 2
    share = weight.shape[0] // n_col
    sparse = (SMEM, SMEM, VMEM)
    adjacency = (tile_coords, tile_counts, adjacency_tiles)

    far = {m: swap(features, "row", m) for m in range(2, n_row, 2)}
    near = swap(features, "row", 1)
    parts = [features, near]
    for m in range(2, n_row, 2):
        parts += [far[m], swap(far[m], "row", 1)]
    cots = [cotangent] + [swap(cotangent, "col", 2 * k) for k in range(1, half)]

    keep, send = call(
        functools.partial(forward_kernel, tile=tile),
        [shape(half * tile, width)] * 2,
        [*sparse, *[VMEM] * n_row],
        [pltpu.VMEM((n_row, tile, width), BF16), pltpu.VMEM((n_col, tile, width), F32)],
    )(*adjacency, *parts)
    other = swap(send, "col", 1)
    partial = call(
        functools.partial(add_kernel, flip=0, tile=tile), shape(half * tile, width), [VMEM] * 2
    )(keep, other)
    bit = 1
    while bit < half:
        other = swap(partial, "col", 2 * bit)
        if 2 * bit < half:
            partial = call(
                functools.partial(add_kernel, flip=bit, tile=tile), shape(half * tile, width), [VMEM] * 2
            )(partial, other)
        bit *= 2

    act, out, kept = call(
        functools.partial(dense_kernel, flip=half // 2, tile=tile, share=share),
        [shape(tile, width), shape(half * tile + share, width), shape(share, width)],
        [VMEM] * (3 + half),
        [pltpu.VMEM((half * tile, width), BF16)] * 2,
    )(partial, other, weight, *cots)
    back = swap(out, "col", 1)

    keep, send = call(
        functools.partial(backward_kernel, tile=tile),
        [shape(n_row // 2 * tile, width)] * 2,
        [*sparse, VMEM, VMEM],
        [pltpu.VMEM((n_col, tile, width), BF16), pltpu.VMEM((n_row, tile, width), F32)],
    )(*adjacency, out, back)
    other = swap(send, "row", 1)

    def total(values, dtype=BF16):
        return call(sum_kernel, shape(*values[0].shape, dtype), [VMEM] * len(values))(*values)

    grad = total([kept, back[half * tile:]])
    grad = total([grad] + [swap(grad, "row", m) for m in range(2, n_row, 2)])
    grad = total([grad, swap(grad, "row", 1)])
    shares = [grad] + [swap(grad, "col", k) for k in range(1, n_col)]
    weight_grad = call(
        functools.partial(place_kernel, share=share),
        shape(*weight.shape, F32),
        [VMEM] * n_col,
    )(*shares)

    pieces = call(
        functools.partial(split_kernel, tile=tile), [shape(tile, width)] * (n_row // 2), [VMEM] * 2
    )(keep, other)
    input_grad = total([pieces[0]] + [swap(p, "row", 2 * k) for k, p in enumerate(pieces) if k])
    return act, weight_grad, input_grad


def solution(mesh):
    return jax.shard_map(
        body,
        mesh=mesh,
        in_specs=(
            P(("row", "col"), None),
            P(),
            P(("row", "col"), None),
            P("row", "col", None, None, None),
            P("row", "col", None, None),
            P("row", "col"),
        ),
        out_specs=(P(("row", "col"), None), P(), P(("row", "col"), None)),
        check_vma=False,
    )
```

```python
import functools

import jax
import jax.numpy as jnp
from jax import lax
from jax.experimental import pallas as pl
from jax.experimental.pallas import tpu as pltpu
from jax.sharding import PartitionSpec as P

F32 = jnp.float32
BF16 = jnp.bfloat16
ANY = pl.BlockSpec(memory_space=pl.ANY)
VMEM = pl.BlockSpec(memory_space=pltpu.VMEM)
SMEM = pl.BlockSpec(memory_space=pltpu.SMEM)
VMEM_LIMIT = 16 * 1024 * 1024
DENSE_LIMIT = 2 * 1024 * 1024
ORDER = lambda n: [0, 1, *range(n - 2, 1, -2)]


def swap(value, row_bits=0, col_bits=0):
    n_row, n_col = lax.axis_size("row"), lax.axis_size("col")
    if not col_bits:
        return lax.ppermute(value, "row", [(i, i ^ row_bits) for i in range(n_row)])
    if not row_bits:
        return lax.ppermute(value, "col", [(j, j ^ col_bits) for j in range(n_col)])
    pairs = [
        (i * n_col + j, (i ^ row_bits) * n_col + (j ^ col_bits)) for i in range(n_row) for j in range(n_col)
    ]
    return lax.ppermute(value, ("row", "col"), pairs)


def call(kernel, outs, in_specs, scratch=(), out_spec=VMEM, us=0.0):
    return pl.pallas_call(
        kernel,
        out_shape=outs,
        in_specs=in_specs,
        out_specs=jax.tree.map(lambda _: out_spec, outs),
        scratch_shapes=list(scratch),
        compiler_params=pltpu.CompilerParams(vmem_limit_bytes=VMEM_LIMIT),
        cost_estimate=pl.CostEstimate(flops=0, bytes_accessed=int(us * 3.69e6), transcendentals=0) if us else None,
    )


def shape(rows, width, dtype=BF16):
    return jax.ShapeDtypeStruct((rows, width), dtype)


def block(ref, k, tile):
    return ref[k * tile:(k + 1) * tile, :]


def place_tiles(coords, count, tiles, *refs, tile, flipped):
    out = refs[-1]
    row, col = lax.axis_index("row"), lax.axis_index("col")
    out[...] = jnp.zeros_like(out)

    def step(s, carry):
        r = pl.multiple_of((coords[0, s] ^ col) * tile, tile)
        c = pl.multiple_of((coords[1, s] ^ row) * tile, tile)
        if flipped:
            out[pl.ds(c, tile), pl.ds(r, tile)] = tiles[0, 0, s].T
        else:
            out[pl.ds(r, tile), pl.ds(c, tile)] = tiles[0, 0, s]
        return carry

    lax.fori_loop(0, count[0, 0], step, 0)


def tile_loop(coords, count, tiles, source, total, flipped, tile):
    row, col = lax.axis_index("row"), lax.axis_index("col")
    total[...] = jnp.zeros_like(total)

    def step(s, carry):
        r = pl.multiple_of((coords[0, s] ^ col) * tile, tile)
        c = pl.multiple_of((coords[1, s] ^ row) * tile, tile)
        if flipped:
            total[pl.ds(c, tile), :] += lax.dot_general(
                tiles[0, 0, s], source[pl.ds(r, tile), :], (((0,), (0,)), ((), ())),
                preferred_element_type=F32,
            )
        else:
            total[pl.ds(r, tile), :] += jnp.dot(
                tiles[0, 0, s], source[pl.ds(c, tile), :], preferred_element_type=F32
            )
        return carry

    lax.fori_loop(0, count[0, 0], step, 0)


def product(adjacency, source, total, flipped, tile):
    if len(adjacency) == 1:
        total[...] = jnp.dot(adjacency[0][...], source[...], preferred_element_type=F32)
    else:
        tile_loop(*adjacency, source, total, flipped, tile)


def split_parity(total, keep, send, tile):
    for k in range(total.shape[0] // (2 * tile)):
        keep[k * tile:(k + 1) * tile, :] = block(total, 2 * k, tile).astype(BF16)
        send[k * tile:(k + 1) * tile, :] = block(total, 2 * k + 1, tile).astype(BF16)


def forward_kernel(*refs, n_adj, slots, tile):
    adjacency, parts = refs[:n_adj], refs[n_adj:n_adj + len(slots)]
    keep, send, source, total = refs[-4:]
    for group, part in zip(slots, parts):
        for n, slot in enumerate(group):
            source[slot * tile:(slot + 1) * tile, :] = block(part, n, tile)
    product(adjacency, source, total, False, tile)
    split_parity(total, keep, send, tile)


def backward_kernel(*refs, n_adj, tile):
    adjacency, (mine, other, kept, keep, send, grad, source, total) = refs[:n_adj], refs[n_adj:]
    for k in range(source.shape[0] // (2 * tile)):
        source[2 * k * tile:(2 * k + 1) * tile, :] = block(mine, k, tile)
        source[(2 * k + 1) * tile:(2 * k + 2) * tile, :] = block(other, k, tile)
    product(adjacency, source, total, True, tile)
    split_parity(total, keep, send, tile)
    rest = source.shape[0] // 2
    grad[...] = (kept[...].astype(F32) + other[rest:, :].astype(F32)).astype(BF16)


def add_kernel(a, b, out, *, flip, tile):
    for k in range(out.shape[0] // tile):
        total = block(a, k, tile).astype(F32) + block(b, k ^ flip, tile).astype(F32)
        out[k * tile:(k + 1) * tile, :] = total.astype(BF16)


def sum_parts(refs):
    total = refs[0][...].astype(F32)
    for ref in refs[1:]:
        total += ref[...].astype(F32)
    return total


def sum_kernel(*refs):
    refs[-1][...] = sum_parts(refs[:-2]).astype(BF16)


def split_kernel(a, b, *outs, tile):
    for k, out in enumerate(outs):
        out[...] = (block(a, k, tile).astype(F32) + block(b, k, tile).astype(F32)).astype(BF16)


def copy_kernel(value, out):
    out[...] = value[...]


def dense_kernel(half, other, weight, *refs, flip, tile, share):
    cots, (act, out, kept, agg, gpre) = refs[:-5], refs[-5:]
    blocks = len(cots)
    add_kernel(half, other, agg, flip=flip, tile=tile)
    col = lax.axis_index("col")
    for k in range(blocks):
        rows = slice(k * tile, (k + 1) * tile)
        pre = jnp.dot(agg[rows, :], weight[...], preferred_element_type=F32)
        sig = jax.nn.sigmoid(pre)
        if k == 0:
            act[...] = (pre * sig).astype(BF16)
        gpre[rows, :] = (cots[k][...].astype(F32) * sig * (1.0 + pre * (1.0 - sig))).astype(BF16)
    grad = lax.dot_general(
        gpre[...], weight[...], (((1,), (1,)), ((), ())), preferred_element_type=F32
    )
    out[:blocks * tile, :] = grad.astype(BF16)
    full = lax.dot_general(
        agg[...], gpre[...], (((0,), (0,)), ((), ())), preferred_element_type=F32
    ).astype(BF16)
    core = col % 2

    @pl.when(core == 0)
    def _():
        kept[...] = full[:share, :]
        out[blocks * tile:, :] = full[share:, :]

    @pl.when(core == 1)
    def _():
        kept[...] = full[share:, :]
        out[blocks * tile:, :] = full[:share, :]


def finish_kernel(act, *refs):
    mine, other, parts = refs[:2], refs[2:4], refs[4:-6]
    act_out, weight_out, input_out, total, grad, sems = refs[-6:]
    core = lax.axis_index("col") % 2
    share = grad.shape[1]
    copies = [pltpu.make_async_copy(act, act_out, sems.at[0])]
    copies[0].start()
    for n, values in enumerate((mine, other)):
        grad[n] = sum_parts(values)
        start = pl.multiple_of((core ^ n) * share, share)
        copies.append(pltpu.make_async_copy(grad.at[n], weight_out.at[pl.ds(start, share), :], sems.at[1 + n]))
        copies[-1].start()
    total[...] = sum_parts(parts).astype(BF16)
    copies.append(pltpu.make_async_copy(total, input_out, sems.at[3]))
    copies[-1].start()
    for copy in copies:
        copy.wait()


def body(features, weight, cotangent, adjacency_tiles, tile_coords, tile_counts):
    tile, width = features.shape
    n_row, n_col = lax.axis_size("row"), lax.axis_size("col")
    half = n_col // 2
    share = weight.shape[0] // 2
    coords = jnp.swapaxes(tile_coords[0, 0], 0, 1)

    def total(values, dtype=BF16):
        return call(sum_kernel, shape(*values[0].shape, dtype), [VMEM] * len(values))(*values)

    parts = {0: features}
    for m in [n_row - 2, *range(2, n_row - 2, 2)]:
        parts[m] = swap(features, m)
        parts[m] = call(copy_kernel, shape(tile, width), [VMEM], us=1.0)(parts[m])
        parts[m + 1] = swap(parts[m], 1)
    parts[1] = swap(features, 1)
    order = list(parts)
    slots, parts = [(m,) for m in order], [parts[m] for m in order]

    dense = n_row * n_col * tile * tile * 2 <= DENSE_LIMIT

    def placed(flipped, *after):
        sides = (n_row, n_col) if flipped else (n_col, n_row)
        return call(
            functools.partial(place_tiles, tile=tile, flipped=flipped),
            shape(sides[0] * tile, sides[1] * tile),
            [SMEM, SMEM, VMEM, *[ANY] * len(after)],
        )(coords, tile_counts, adjacency_tiles, *after)

    ahead = back = (coords, tile_counts, adjacency_tiles)
    specs = [SMEM, SMEM, VMEM]
    if dense:
        ahead, back, specs = (placed(False),), (placed(True),), [VMEM]

    cots = [cotangent] + [swap(cotangent, 0, 2 * k) for k in range(1, half)]
    keep, send = call(
        functools.partial(forward_kernel, n_adj=len(specs), slots=slots, tile=tile),
        [shape(half * tile, width)] * 2,
        [*specs, *[VMEM] * len(parts), *[ANY] * (half - 1)],
        [pltpu.VMEM((n_row * tile, width), BF16), pltpu.VMEM((n_col * tile, width), F32)],
    )(*ahead, *parts, *cots[1:])
    other = swap(send, 0, 1)
    partial = call(
        functools.partial(add_kernel, flip=0, tile=tile), shape(half * tile, width), [VMEM] * 2
    )(keep, other)
    bit = 1
    while bit < half:
        other = swap(partial, 0, 2 * bit)
        if 2 * bit < half:
            partial = call(
                functools.partial(add_kernel, flip=bit, tile=tile), shape(half * tile, width), [VMEM] * 2
            )(partial, other)
        bit *= 2
    act, out, kept = call(
        functools.partial(dense_kernel, flip=half // 2, tile=tile, share=share),
        [shape(tile, width), shape(half * tile + share, width), shape(share, width)],
        [VMEM] * (3 + half),
        [pltpu.VMEM((half * tile, width), BF16)] * 2,
    )(partial, other, weight, *cots)
    other = swap(out, 0, 1)

    keep, send, grad = call(
        functools.partial(backward_kernel, n_adj=len(specs), tile=tile),
        [shape(n_row // 2 * tile, width)] * 2 + [shape(share, width)],
        [*specs, VMEM, VMEM, VMEM],
        [pltpu.VMEM((n_col * tile, width), BF16), pltpu.VMEM((n_row * tile, width), F32)],
    )(*back, out, other, kept)
    other = swap(send, 1)
    grads = [grad] + [swap(grad, m) for m in range(2, n_row, 2)]
    pieces = call(
        functools.partial(split_kernel, tile=tile), [shape(tile, width)] * (n_row // 2), [VMEM] * 2
    )(keep, other)
    arrived = [pieces[0]] + [swap(pieces[k], 2 * k) for k in range(n_row // 2 - 1, 0, -1)]
    grad = call(sum_kernel, shape(share, width), [VMEM] * len(grads) + [ANY])(
        *grads, arrived[-1]
    )
    grads = [grad, swap(grad, 1), swap(grad, 0, 1), swap(grad, 1, 1)]
    return call(
        finish_kernel,
        [shape(tile, width), shape(*weight.shape, F32), shape(tile, width)],
        [VMEM] * (1 + len(grads) + len(arrived)),
        [pltpu.VMEM((tile, width), BF16), pltpu.VMEM((2, share, width), F32), pltpu.SemaphoreType.DMA((4,))],
        ANY,
    )(act, *grads, *arrived)


def solution(mesh):
    return jax.shard_map(
        body,
        mesh=mesh,
        in_specs=(
            P(("row", "col"), None),
            P(),
            P(("row", "col"), None),
            P("row", "col", None, None, None),
            P("row", "col", None, None),
            P("row", "col"),
        ),
        out_specs=(P(("row", "col"), None), P(), P(("row", "col"), None)),
        check_vma=False,
    )
```

```python
import functools

import jax
import jax.numpy as jnp
from jax import lax
from jax.experimental import pallas as pl
from jax.experimental.pallas import tpu as pltpu
from jax.sharding import PartitionSpec as P

F32 = jnp.float32
BF16 = jnp.bfloat16
ANY = pl.BlockSpec(memory_space=pl.ANY)
VMEM = pl.BlockSpec(memory_space=pltpu.VMEM)
SMEM = pl.BlockSpec(memory_space=pltpu.SMEM)
VMEM_LIMIT = 16 * 1024 * 1024
DENSE_LIMIT = 2 * 1024 * 1024


def swap(value, row_bits=0, col_bits=0):
    n_row, n_col = lax.axis_size("row"), lax.axis_size("col")
    if not col_bits:
        return lax.ppermute(value, "row", [(i, i ^ row_bits) for i in range(n_row)])
    if not row_bits:
        return lax.ppermute(value, "col", [(j, j ^ col_bits) for j in range(n_col)])
    pairs = [
        (i * n_col + j, (i ^ row_bits) * n_col + (j ^ col_bits)) for i in range(n_row) for j in range(n_col)
    ]
    return lax.ppermute(value, ("row", "col"), pairs)


def call(kernel, outs, in_specs, scratch=(), out_spec=VMEM, us=0.0):
    return pl.pallas_call(
        kernel,
        out_shape=outs,
        in_specs=in_specs,
        out_specs=jax.tree.map(lambda _: out_spec, outs),
        scratch_shapes=list(scratch),
        compiler_params=pltpu.CompilerParams(vmem_limit_bytes=VMEM_LIMIT),
        cost_estimate=pl.CostEstimate(flops=0, bytes_accessed=int(us * 3.69e6), transcendentals=0) if us else None,
    )


def shape(rows, width, dtype=BF16):
    return jax.ShapeDtypeStruct((rows, width), dtype)


def block(ref, k, tile):
    return ref[k * tile:(k + 1) * tile, :]


def place_tiles(coords, count, tiles, *refs, tile, flipped):
    out = refs[-1]
    row, col = lax.axis_index("row"), lax.axis_index("col")
    out[...] = jnp.zeros_like(out)

    def step(s, carry):
        r = pl.multiple_of((coords[0, s] ^ col) * tile, tile)
        c = pl.multiple_of((coords[1, s] ^ row) * tile, tile)
        if flipped:
            out[pl.ds(c, tile), pl.ds(r, tile)] = tiles[0, 0, s].T
        else:
            out[pl.ds(r, tile), pl.ds(c, tile)] = tiles[0, 0, s]
        return carry

    lax.fori_loop(0, count[0, 0], step, 0)


def tile_loop(coords, count, tiles, source, total, flipped, tile):
    row, col = lax.axis_index("row"), lax.axis_index("col")
    total[...] = jnp.zeros_like(total)

    def step(s, carry):
        r = pl.multiple_of((coords[0, s] ^ col) * tile, tile)
        c = pl.multiple_of((coords[1, s] ^ row) * tile, tile)
        if flipped:
            total[pl.ds(c, tile), :] += lax.dot_general(
                tiles[0, 0, s], source[pl.ds(r, tile), :], (((0,), (0,)), ((), ())),
                preferred_element_type=F32,
            )
        else:
            total[pl.ds(r, tile), :] += jnp.dot(
                tiles[0, 0, s], source[pl.ds(c, tile), :], preferred_element_type=F32
            )
        return carry

    lax.fori_loop(0, count[0, 0], step, 0)


def product(adjacency, source, total, flipped, tile):
    if len(adjacency) == 1:
        total[...] = jnp.dot(adjacency[0][...], source[...], preferred_element_type=F32)
    else:
        tile_loop(*adjacency, source, total, flipped, tile)


def split_parity(total, keep, send, tile):
    for k in range(total.shape[0] // (2 * tile)):
        keep[k * tile:(k + 1) * tile, :] = block(total, 2 * k, tile).astype(BF16)
        send[k * tile:(k + 1) * tile, :] = block(total, 2 * k + 1, tile).astype(BF16)


def forward_kernel(*refs, n_adj, slots, tile):
    adjacency, parts = refs[:n_adj], refs[n_adj:n_adj + len(slots)]
    keep, send, source, total = refs[-4:]
    for group, part in zip(slots, parts):
        for n, slot in enumerate(group):
            source[slot * tile:(slot + 1) * tile, :] = block(part, n, tile)
    product(adjacency, source, total, False, tile)
    split_parity(total, keep, send, tile)


def backward_kernel(*refs, n_adj, tile):
    adjacency, (mine, other, kept, keep, keep_far, send, send_far, grad, source, total) = refs[:n_adj], refs[n_adj:]
    for k in range(source.shape[0] // (2 * tile)):
        source[2 * k * tile:(2 * k + 1) * tile, :] = block(mine, k, tile)
        source[(2 * k + 1) * tile:(2 * k + 2) * tile, :] = block(other, k, tile)
    product(adjacency, source, total, True, tile)
    rows = total.shape[0] // 2
    split_parity(total.at[rows:, :], keep_far, send_far, tile)
    split_parity(total.at[:rows, :], keep, send, tile)
    rest = source.shape[0] // 2
    grad[...] = (kept[...].astype(F32) + other[rest:, :].astype(F32)).astype(BF16)


def add_kernel(a, b, out, *, flip, tile):
    for k in range(out.shape[0] // tile):
        total = block(a, k, tile).astype(F32) + block(b, k ^ flip, tile).astype(F32)
        out[k * tile:(k + 1) * tile, :] = total.astype(BF16)


def sum_parts(refs):
    total = refs[0][...].astype(F32)
    for ref in refs[1:]:
        total += ref[...].astype(F32)
    return total


def sum_kernel(*refs, n):
    refs[-1][...] = sum_parts(refs[:n]).astype(BF16)


def split_kernel(a, b, *outs, tile):
    for k, out in enumerate(outs):
        out[...] = (block(a, k, tile).astype(F32) + block(b, k, tile).astype(F32)).astype(BF16)


def copy_kernel(value, out):
    out[...] = value[...]


def dense_kernel(half, other, weight, *refs, flip, tile, share):
    cots, (act, out, kept, agg, gpre) = refs[:-5], refs[-5:]
    blocks = len(cots)
    add_kernel(half, other, agg, flip=flip, tile=tile)
    col = lax.axis_index("col")
    for k in range(blocks):
        rows = slice(k * tile, (k + 1) * tile)
        pre = jnp.dot(agg[rows, :], weight[...], preferred_element_type=F32)
        sig = jax.nn.sigmoid(pre)
        if k == 0:
            act[...] = (pre * sig).astype(BF16)
        gpre[rows, :] = (cots[k][...].astype(F32) * sig * (1.0 + pre * (1.0 - sig))).astype(BF16)
    grad = lax.dot_general(
        gpre[...], weight[...], (((1,), (1,)), ((), ())), preferred_element_type=F32
    )
    out[:blocks * tile, :] = grad.astype(BF16)
    full = lax.dot_general(
        agg[...], gpre[...], (((0,), (0,)), ((), ())), preferred_element_type=F32
    ).astype(BF16)
    core = col % 2

    @pl.when(core == 0)
    def _():
        kept[...] = full[:share, :]
        out[blocks * tile:, :] = full[share:, :]

    @pl.when(core == 1)
    def _():
        kept[...] = full[share:, :]
        out[blocks * tile:, :] = full[:share, :]


def finish_kernel(act, *refs):
    mine, other, parts = refs[:2], refs[2:4], refs[4:-6]
    act_out, weight_out, input_out, total, grad, sems = refs[-6:]
    core = lax.axis_index("col") % 2
    share = grad.shape[1]
    copies = [pltpu.make_async_copy(act, act_out, sems.at[0])]
    copies[0].start()
    for n, values in enumerate((mine, other)):
        grad[n] = sum_parts(values)
        start = pl.multiple_of((core ^ n) * share, share)
        copies.append(pltpu.make_async_copy(grad.at[n], weight_out.at[pl.ds(start, share), :], sems.at[1 + n]))
        copies[-1].start()
    total[...] = sum_parts(parts).astype(BF16)
    copies.append(pltpu.make_async_copy(total, input_out, sems.at[3]))
    copies[-1].start()
    for copy in copies:
        copy.wait()


def body(features, weight, cotangent, adjacency_tiles, tile_coords, tile_counts):
    tile, width = features.shape
    n_row, n_col = lax.axis_size("row"), lax.axis_size("col")
    half = n_col // 2
    share = weight.shape[0] // 2
    coords = jnp.swapaxes(tile_coords[0, 0], 0, 1)

    parts = {0: features}
    for m in [n_row - 2, *range(2, n_row - 2, 2)]:
        parts[m] = swap(features, m)
        parts[m] = call(copy_kernel, shape(tile, width), [VMEM], us=1.0)(parts[m])
        parts[m + 1] = swap(parts[m], 1)
    parts[1] = swap(features, 1)
    order = list(parts)
    slots, parts = [(m,) for m in order], [parts[m] for m in order]

    dense = n_row * n_col * tile * tile * 2 <= DENSE_LIMIT

    def placed(flipped):
        sides = (n_row, n_col) if flipped else (n_col, n_row)
        return call(
            functools.partial(place_tiles, tile=tile, flipped=flipped),
            shape(sides[0] * tile, sides[1] * tile),
            [SMEM, SMEM, VMEM],
        )(coords, tile_counts, adjacency_tiles)

    ahead = back = (coords, tile_counts, adjacency_tiles)
    specs = [SMEM, SMEM, VMEM]
    if dense:
        ahead, back, specs = (placed(False),), (placed(True),), [VMEM]

    cots = [cotangent] + [swap(cotangent, 0, 2 * k) for k in range(1, half)]
    keep, send = call(
        functools.partial(forward_kernel, n_adj=len(specs), slots=slots, tile=tile),
        [shape(half * tile, width)] * 2,
        [*specs, *[VMEM] * len(parts), *[ANY] * (half - 1)],
        [pltpu.VMEM((n_row * tile, width), BF16), pltpu.VMEM((n_col * tile, width), F32)],
    )(*ahead, *parts, *cots[1:])
    other = swap(send, 0, 1)
    partial = call(
        functools.partial(add_kernel, flip=0, tile=tile), shape(half * tile, width), [VMEM] * 2
    )(keep, other)
    bit = 1
    while bit < half:
        other = swap(partial, 0, 2 * bit)
        if 2 * bit < half:
            partial = call(
                functools.partial(add_kernel, flip=bit, tile=tile), shape(half * tile, width), [VMEM] * 2
            )(partial, other)
        bit *= 2
    act, out, kept = call(
        functools.partial(dense_kernel, flip=half // 2, tile=tile, share=share),
        [shape(tile, width), shape(half * tile + share, width), shape(share, width)],
        [VMEM] * (3 + half),
        [pltpu.VMEM((half * tile, width), BF16)] * 2,
    )(partial, other, weight, *cots)
    other = swap(out, 0, 1)

    near, far, send, send_far, grad = call(
        functools.partial(backward_kernel, n_adj=len(specs), tile=tile),
        [shape(n_row // 4 * tile, width)] * 4 + [shape(share, width)],
        [*specs, VMEM, VMEM, VMEM],
        [pltpu.VMEM((n_col * tile, width), BF16), pltpu.VMEM((n_row * tile, width), F32)],
    )(*back, out, other, kept)
    far_other = swap(send_far, 1)
    other = swap(send, 1)
    grads = [grad] + [swap(grad, m) for m in range(2, n_row, 2)]
    halves = [
        call(functools.partial(split_kernel, tile=tile), [shape(tile, width)] * (n_row // 4), [VMEM] * 2)(*pair)
        for pair in ((near, other), (far, far_other))
    ]
    pieces = [*halves[0], *halves[1]]
    arrived = [pieces[0]] + [swap(pieces[k], 2 * k) for k in [*range(2, n_row // 2), 1]]
    grad = call(functools.partial(sum_kernel, n=len(grads)), shape(share, width), [VMEM] * len(grads) + [ANY])(
        *grads, arrived[-1]
    )
    grads = [grad, swap(grad, 1), swap(grad, 0, 1), swap(grad, 1, 1)]
    return call(
        finish_kernel,
        [shape(tile, width), shape(*weight.shape, F32), shape(tile, width)],
        [VMEM] * (1 + len(grads) + len(arrived)),
        [pltpu.VMEM((tile, width), BF16), pltpu.VMEM((2, share, width), F32), pltpu.SemaphoreType.DMA((4,))],
        ANY,
    )(act, *grads, *arrived)


def solution(mesh):
    return jax.shard_map(
        body,
        mesh=mesh,
        in_specs=(
            P(("row", "col"), None),
            P(),
            P(("row", "col"), None),
            P("row", "col", None, None, None),
            P("row", "col", None, None),
            P("row", "col"),
        ),
        out_specs=(P(("row", "col"), None), P(), P(("row", "col"), None)),
        check_vma=False,
    )
```
